32 devices in a mesh: rep: 2 (over x), gx: 16 (over z, y, core).
Axes of the slice: x: 2, y: 2, z: 4, core: 2. Of those that a mesh axis runs over, the one named last changes fastest.
Arguments:
- in_field: bfloat16 [64, 16, 64, 128], P(('rep', 'gx')), parts along dimension 0, may hold values from -6 to 6
- cotangent: bfloat16 [64, 16, 64, 128], P(('rep', 'gx')), parts along dimension 0, may hold values from -6 to 6
- spec_weight: bfloat16 [256, 64, 128], P('gx'), may hold values from -4 to 4
- w_in: bfloat16 [64, 128], replicated, may hold values from -0.75 to 0.75
- w_out: bfloat16 [128, 64], replicated, may hold values from -0.5 to 0.5
Outputs:
- grad_field: bfloat16 [64, 16, 64, 128], P(('rep', 'gx')), parts along dimension 0
- grad_spec: float32 [512, 64, 128], P(('rep', 'gx')), parts along dimension 0
- grad_w_in: float32 [128, 128], P('rep'), parts along dimension 0
- grad_w_out: float32 [256, 64], P('rep'), parts along dimension 0
The draws below stay inside these ranges and needn't reach their ends.
There are 2 independent parts, one for each index of `rep`. The reference program is written for one: setup_inputs(seed, part) draws one part's arguments, and reference() takes and returns one part's arrays. A program takes and returns all parts, laid end to end along the dimension named above; an argument that names none is the same for every part. Nothing has to cross between parts.
All inputs are finite; a program needn't handle non-finite values.
Results may differ from the reference program's by a relative error of at most 0.01.
Values may be sent and summed in bfloat16 or wider, within the bound.
A program may use at most 128 MiB of HBM per device.

```python
import math
import jax
import jax.numpy as jnp
from jax import lax

C = 64
H = 128
NZ = 128
KZ = 16
KX = 16
NX = 32
NY = 16
MODES = 256


def steps_of(stream_key, shape, shards, low, high):
    gain = 1.0
    for dim, parts in shards:
        heights = jax.random.uniform(jax.random.fold_in(jax.random.fold_in(stream_key, 6), dim), (parts,), jnp.float32, low / len(shards), high / len(shards))
        gain = gain * jnp.repeat(jnp.exp(heights), shape[dim] // parts).reshape((-1,) + (1,) * (len(shape) - 1 - dim))
    return gain


def centred(own_key, dims, spread, most, cuts=(), held_as=jnp.bfloat16):
    gain = steps_of(own_key, dims, cuts, -0.22, 0.18) if cuts else 1.0
    values = jax.random.normal(own_key, dims, jnp.float32) * spread * gain
    return jnp.minimum(jnp.maximum(values, -most), most).astype(held_as)


def setup_inputs(seed: int = 0, part: int = 0) -> dict:
    seeds = jax.random.split(jax.random.key(seed), 6)
    own_keys = jax.random.split(jax.random.fold_in(seeds[5], part), 6)
    in_field = centred(own_keys[0], (NX, NY, C, NZ), 1.0, 6.0, ((0, 16),))
    cotangent = centred(own_keys[1], (NX, NY, C, NZ), 1.0, 6.0, ((0, 16),))
    spec_weight = centred(seeds[2], (MODES, C, 2 * C), 0.25, 4.0, ((0, 16),))
    w_in = centred(seeds[3], (C, H), C ** -0.5, 0.75)
    w_out = centred(seeds[4], (H, C), H ** -0.5, 0.5)
    return dict(in_field=in_field, cotangent=cotangent, spec_weight=spec_weight, w_in=w_in, w_out=w_out)


def make_tables(length_x, length_z):
    z_pos = jnp.arange(length_z, dtype=jnp.int32)
    k_z = jnp.arange(KZ, dtype=jnp.int32)
    angle_z = 2.0 * math.pi * (k_z[:, None] * z_pos[None, :] % length_z).astype(jnp.float32) / length_z
    cos_z = jnp.cos(angle_z)
    sin_z = jnp.sin(angle_z)
    k_weight = jnp.where(k_z == 0, 1.0, 2.0).astype(jnp.float32)[:, None]
    forward_z = (jnp.concatenate([cos_z, -sin_z], 0).T / math.sqrt(length_z)).astype(jnp.bfloat16)
    inverse_z = (jnp.concatenate([k_weight * cos_z, -k_weight * sin_z], 0) / math.sqrt(length_z)).astype(jnp.bfloat16)
    j_index = jnp.arange(KX, dtype=jnp.int32)
    k_x = jnp.where(j_index < KX // 2, j_index, length_x - KX + j_index)
    x_pos = jnp.arange(length_x, dtype=jnp.int32)
    angle_x = 2.0 * math.pi * (k_x[:, None] * x_pos[None, :] % length_x).astype(jnp.float32) / length_x
    cosine_x = jnp.cos(angle_x) / math.sqrt(length_x)
    sine_x = jnp.sin(angle_x) / math.sqrt(length_x)
    return (forward_z, inverse_z, cosine_x, sine_x)

def x_forward(pencil, cosine_x, sine_x):
    data = pencil.astype(jnp.float32)
    cos_b = cosine_x.astype(jnp.bfloat16).astype(jnp.float32)
    sin_b = sine_x.astype(jnp.bfloat16).astype(jnp.float32)
    real_part = data[..., :KZ]
    imag_part = data[..., KZ:]
    out_real = jnp.einsum('jx,xyck->yjkc', cos_b, real_part) + jnp.einsum('jx,xyck->yjkc', sin_b, imag_part)
    out_imag = jnp.einsum('jx,xyck->yjkc', cos_b, imag_part) - jnp.einsum('jx,xyck->yjkc', sin_b, real_part)
    joined = jnp.concatenate([out_real, out_imag], -1)
    return joined.reshape(joined.shape[0], KX * KZ, joined.shape[-1])

def x_inverse(spectrum, cosine_x, sine_x):
    rows = spectrum.shape[0]
    chans = spectrum.shape[-1] // 2
    shaped = spectrum.reshape(rows, KX, KZ, 2 * chans)
    real_part = shaped[..., :chans]
    imag_part = shaped[..., chans:]
    high = lax.Precision.HIGHEST
    out_real = jnp.einsum('jx,yjkc->xyck', cosine_x, real_part, precision=high) - jnp.einsum('jx,yjkc->xyck', sine_x, imag_part, precision=high)
    out_imag = jnp.einsum('jx,yjkc->xyck', cosine_x, imag_part, precision=high) + jnp.einsum('jx,yjkc->xyck', sine_x, real_part, precision=high)
    return jnp.concatenate([out_real, out_imag], -1)

def mixing(spectrum, weight):
    chans = weight.shape[1]
    high = lax.Precision.HIGHEST
    prod_real = jnp.einsum('ymc,mcf->ymf', spectrum[..., :chans], weight, precision=high)
    prod_imag = jnp.einsum('ymc,mcf->ymf', spectrum[..., chans:], weight, precision=high)
    return jnp.concatenate([prod_real[..., :chans] - prod_imag[..., chans:], prod_real[..., chans:] + prod_imag[..., :chans]], -1)

def mixing_back(d_spectrum, spectrum, weight):
    chans = weight.shape[1]
    high = lax.Precision.HIGHEST
    d_real = d_spectrum[..., :chans]
    d_imag = d_spectrum[..., chans:]
    d_cat = jnp.concatenate([d_real, d_imag], -1)
    d_rot = jnp.concatenate([d_imag, -d_real], -1)
    d_xr = jnp.einsum('ymf,mcf->ymc', d_cat, weight, precision=high)
    d_xi = jnp.einsum('ymf,mcf->ymc', d_rot, weight, precision=high)
    grads = jnp.einsum('ymc,ymf->mcf', spectrum[..., :chans], d_cat, precision=high)
    grads = grads + jnp.einsum('ymc,ymf->mcf', spectrum[..., chans:], d_rot, precision=high)
    return (jnp.concatenate([d_xr, d_xi], -1), grads)

def pointwise(in_slab, cot_slab, inverse_b, w_in, w_out, inverse_z):
    f32 = jnp.float32
    spectral = jnp.einsum('...ck,kz->...cz', inverse_b.astype(f32), inverse_z.astype(f32))
    hidden = jnp.einsum('...cz,ch->...hz', in_slab.astype(f32), w_in.astype(f32))
    act_b = jax.nn.gelu(hidden).astype(jnp.bfloat16)
    branch = jnp.einsum('...hz,hc->...cz', act_b.astype(f32), w_out.astype(f32))
    pre = spectral + branch
    unused_t, pull_t = jax.vjp(jax.nn.gelu, pre)
    d_pre = pull_t(cot_slab.astype(f32))[0].astype(jnp.bfloat16)
    d_hidden = jnp.einsum('...cz,hc->...hz', d_pre.astype(f32), w_out.astype(f32))
    unused_h, pull_h = jax.vjp(jax.nn.gelu, hidden)
    d_act = pull_h(d_hidden)[0].astype(jnp.bfloat16)
    du_mlp = jnp.einsum('...hz,ch->...cz', d_act.astype(f32), w_in.astype(f32))
    dw_out = jnp.einsum('...hz,...cz->hc', act_b.astype(f32), d_pre.astype(f32))
    dw_in = jnp.einsum('...cz,...hz->ch', in_slab.astype(f32), d_act.astype(f32))
    d_inverse = jnp.einsum('...cz,kz->...ck', d_pre.astype(f32), inverse_z.astype(f32)).astype(jnp.bfloat16)
    return (d_inverse, du_mlp, dw_in, dw_out)

def reference(in_field, cotangent, spec_weight, w_in, w_out):
    f32 = jnp.float32
    forward_z, inverse_z, cosine_x, sine_x = make_tables(NX, NZ)

    def z_coeffs(one_plane):
        return jnp.einsum('ycz,zk->yck', one_plane.astype(f32), forward_z.astype(f32)).astype(jnp.bfloat16)
    coeffs = lax.map(z_coeffs, in_field)
    spectrum = x_forward(coeffs, cosine_x, sine_x)
    weight_f = spec_weight.astype(f32)
    mixed = mixing(spectrum, weight_f)
    inverse_b = x_inverse(mixed, cosine_x, sine_x).astype(jnp.bfloat16)

    def one_step(carry, pieces):
        d_inverse, du_mlp, dw_in, dw_out = pointwise(pieces[0], pieces[1], pieces[2], w_in, w_out, inverse_z)
        return ((carry[0] + dw_in, carry[1] + dw_out), (d_inverse, du_mlp))
    start = (jnp.zeros((C, H), f32), jnp.zeros((H, C), f32))
    sums, outs = lax.scan(one_step, start, (in_field, cotangent, inverse_b))
    d_inverse, du_mlp = outs
    d_mixed = x_forward(d_inverse, cosine_x, sine_x)
    d_spectrum, grad_spec = mixing_back(d_mixed, spectrum, weight_f)
    d_coeffs = x_inverse(d_spectrum, cosine_x, sine_x).astype(jnp.bfloat16)

    def finish(pieces):
        du_spec = jnp.einsum('yck,zk->ycz', pieces[0].astype(f32), forward_z.astype(f32))
        return (du_spec + pieces[1]).astype(jnp.bfloat16)
    grad_field = lax.map(finish, (d_coeffs, du_mlp))
    grad_scale = 1.0 / math.sqrt(NX * NY * NZ)
    return (grad_field, grad_spec, sums[0] * grad_scale, sums[1] * grad_scale)
```

```python
import math

import jax
import jax.numpy as jnp
from jax import lax
from jax.sharding import PartitionSpec as P

KZ = 16
KX = 16


def make_tables(length_x, length_z):
    z_pos = jnp.arange(length_z, dtype=jnp.int32)
    k_z = jnp.arange(KZ, dtype=jnp.int32)
    angle_z = (
        2.0 * math.pi * (k_z[:, None] * z_pos[None, :] % length_z).astype(jnp.float32) / length_z
    )
    cos_z = jnp.cos(angle_z)
    sin_z = jnp.sin(angle_z)
    k_weight = jnp.where(k_z == 0, 1.0, 2.0).astype(jnp.float32)[:, None]
    forward_z = (jnp.concatenate([cos_z, -sin_z], 0).T / math.sqrt(length_z)).astype(jnp.bfloat16)
    inverse_z = (
        jnp.concatenate([k_weight * cos_z, -k_weight * sin_z], 0) / math.sqrt(length_z)
    ).astype(jnp.bfloat16)
    j_index = jnp.arange(KX, dtype=jnp.int32)
    k_x = jnp.where(j_index < KX // 2, j_index, length_x - KX + j_index)
    x_pos = jnp.arange(length_x, dtype=jnp.int32)
    angle_x = (
        2.0 * math.pi * (k_x[:, None] * x_pos[None, :] % length_x).astype(jnp.float32) / length_x
    )
    cosine_x = jnp.cos(angle_x) / math.sqrt(length_x)
    sine_x = jnp.sin(angle_x) / math.sqrt(length_x)
    return (forward_z, inverse_z, cosine_x, sine_x)


def x_halves(pencil, cos_b, sin_b):
    f32 = jnp.float32
    real_part = pencil[..., :KZ]
    imag_part = pencil[..., KZ:]
    out_real = jnp.einsum(
        "jx,xyck->yjkc", cos_b, real_part, preferred_element_type=f32
    ) + jnp.einsum("jx,xyck->yjkc", sin_b, imag_part, preferred_element_type=f32)
    out_imag = jnp.einsum(
        "jx,xyck->yjkc", cos_b, imag_part, preferred_element_type=f32
    ) - jnp.einsum("jx,xyck->yjkc", sin_b, real_part, preferred_element_type=f32)
    return (out_real, out_imag)


def join_halves(halves):
    joined = jnp.concatenate([halves[0], halves[1]], -1)
    return joined.reshape(joined.shape[0], KX * KZ, joined.shape[-1])


def x_inverse(spectrum, cosine_x, sine_x):
    rows = spectrum.shape[0]
    chans = spectrum.shape[-1] // 2
    shaped = spectrum.reshape(rows, KX, KZ, 2 * chans)
    real_part = shaped[..., :chans]
    imag_part = shaped[..., chans:]
    high = lax.Precision.HIGHEST
    out_real = jnp.einsum("jx,yjkc->xyck", cosine_x, real_part, precision=high) - jnp.einsum(
        "jx,yjkc->xyck", sine_x, imag_part, precision=high
    )
    out_imag = jnp.einsum("jx,yjkc->xyck", cosine_x, imag_part, precision=high) + jnp.einsum(
        "jx,yjkc->xyck", sine_x, real_part, precision=high
    )
    return jnp.concatenate([out_real, out_imag], -1)


def mixing(spectrum, weight):
    chans = weight.shape[1]
    high = lax.Precision.HIGHEST
    prod_real = jnp.einsum("ymc,mcf->ymf", spectrum[..., :chans], weight, precision=high)
    prod_imag = jnp.einsum("ymc,mcf->ymf", spectrum[..., chans:], weight, precision=high)
    return jnp.concatenate(
        [
            prod_real[..., :chans] - prod_imag[..., chans:],
            prod_real[..., chans:] + prod_imag[..., :chans],
        ],
        -1,
    )


def mixing_back(d_spectrum, spectrum, weight):
    chans = weight.shape[1]
    high = lax.Precision.HIGHEST
    d_real = d_spectrum[..., :chans]
    d_imag = d_spectrum[..., chans:]
    d_cat = jnp.concatenate([d_real, d_imag], -1)
    d_rot = jnp.concatenate([d_imag, -d_real], -1)
    d_xr = jnp.einsum("ymf,mcf->ymc", d_cat, weight, precision=high)
    d_xi = jnp.einsum("ymf,mcf->ymc", d_rot, weight, precision=high)
    grads = jnp.einsum("ymc,ymf->mcf", spectrum[..., :chans], d_cat, precision=high)
    grads = grads + jnp.einsum("ymc,ymf->mcf", spectrum[..., chans:], d_rot, precision=high)
    return (jnp.concatenate([d_xr, d_xi], -1), grads)


def pointwise(in_slab, cot_slab, inverse_b, w_in, w_out, inverse_z):
    f32 = jnp.float32
    spectral = jnp.einsum("xyck,kz->xycz", inverse_b, inverse_z, preferred_element_type=f32)
    hidden = jnp.einsum("xycz,ch->xyhz", in_slab, w_in, preferred_element_type=f32)
    act_b = jax.nn.gelu(hidden).astype(jnp.bfloat16)
    branch = jnp.einsum("xyhz,hc->xycz", act_b, w_out, preferred_element_type=f32)
    pre = spectral + branch
    unused_t, pull_t = jax.vjp(jax.nn.gelu, pre)
    d_pre = pull_t(cot_slab.astype(f32))[0].astype(jnp.bfloat16)
    d_hidden = jnp.einsum("xycz,hc->xyhz", d_pre, w_out, preferred_element_type=f32)
    unused_h, pull_h = jax.vjp(jax.nn.gelu, hidden)
    d_act = pull_h(d_hidden)[0].astype(jnp.bfloat16)
    du_mlp = jnp.einsum("xyhz,ch->xycz", d_act, w_in, preferred_element_type=f32)
    dw_out = jnp.einsum("xyhz,xycz->hc", act_b, d_pre, preferred_element_type=f32)
    dw_in = jnp.einsum("xycz,xyhz->ch", in_slab, d_act, preferred_element_type=f32)
    d_inverse = jnp.einsum("xycz,kz->xyck", d_pre, inverse_z, preferred_element_type=f32).astype(
        jnp.bfloat16
    )
    return (d_inverse, du_mlp, dw_in, dw_out)


def body(in_field, cotangent, spec_weight, w_in, w_out):
    f32 = jnp.float32
    devices_x = lax.axis_size("gx")
    planes = in_field.shape[0]
    rows_all = in_field.shape[1]
    z_cells = in_field.shape[3]
    length_x = planes * devices_x
    forward_z, inverse_z, cosine_x, sine_x = make_tables(length_x, z_cells)
    cos_b = cosine_x.astype(jnp.bfloat16)
    sin_b = sine_x.astype(jnp.bfloat16)

    def transform_x(pencil):
        return x_halves(pencil, cos_b, sin_b)

    coeffs = jnp.einsum("xycz,zk->xyck", in_field, forward_z, preferred_element_type=f32).astype(
        jnp.bfloat16
    )
    pencil = lax.all_to_all(coeffs, "gx", split_axis=1, concat_axis=0, tiled=True)
    spectrum = join_halves(transform_x(pencil))
    owned_spec = lax.all_to_all(spectrum, "gx", split_axis=1, concat_axis=0, tiled=True)
    weight_f = spec_weight.astype(f32)
    returned = lax.all_to_all(
        mixing(owned_spec, weight_f), "gx", split_axis=0, concat_axis=1, tiled=True
    )
    inverse_b = x_inverse(returned, cosine_x, sine_x).astype(jnp.bfloat16)
    back_slabs = lax.all_to_all(inverse_b, "gx", split_axis=0, concat_axis=1, tiled=True)
    d_inverse, du_mlp, dw_in, dw_out = pointwise(
        in_field, cotangent, back_slabs, w_in, w_out, inverse_z
    )
    grad_pencil = lax.all_to_all(d_inverse, "gx", split_axis=1, concat_axis=0, tiled=True)
    d_mixed = join_halves(transform_x(grad_pencil))
    chans = dw_in.shape[0]
    lanes = 2 * chans
    parts = jnp.concatenate([dw_in.reshape(-1, lanes), dw_out.reshape(-1, lanes)], 0)
    parts = parts.reshape(devices_x, -1, lanes)
    own_modes = spec_weight.shape[0]
    rows_own = d_mixed.shape[0]
    send = jnp.concatenate(
        [
            d_mixed.reshape(rows_own, devices_x, own_modes, lanes)
            .transpose(1, 0, 2, 3)
            .reshape(devices_x, rows_own * own_modes, lanes),
            parts,
        ],
        1,
    )
    got = lax.all_to_all(send, "gx", split_axis=0, concat_axis=0, tiled=True)
    d_owned = got[:, : rows_own * own_modes].reshape(rows_all, own_modes, lanes)
    reduced = jnp.sum(got[:, rows_own * own_modes :], 0)
    d_local, grad_spec = mixing_back(d_owned, owned_spec, weight_f)
    send = jnp.concatenate(
        [
            d_local.reshape(devices_x, rows_own * own_modes, lanes),
            jnp.broadcast_to(reduced[None], (devices_x,) + reduced.shape),
        ],
        1,
    )
    got = lax.all_to_all(send, "gx", split_axis=0, concat_axis=0, tiled=True)
    d_returned = (
        got[:, : rows_own * own_modes]
        .reshape(devices_x, rows_own, own_modes, lanes)
        .transpose(1, 0, 2, 3)
        .reshape(rows_own, devices_x * own_modes, lanes)
    )
    summed = got[:, rows_own * own_modes :].reshape(-1, lanes)
    dw_in, dw_out = summed[:chans], summed[chans:].reshape(dw_out.shape)
    d_coeffs = x_inverse(d_returned, cosine_x, sine_x).astype(jnp.bfloat16)
    grad_slabs = lax.all_to_all(d_coeffs, "gx", split_axis=0, concat_axis=1, tiled=True)
    du_spec = jnp.einsum("xyck,zk->xycz", grad_slabs, forward_z, preferred_element_type=f32)
    grad_field = (du_spec + du_mlp).astype(jnp.bfloat16)
    grad_scale = 1.0 / math.sqrt(length_x * rows_all * z_cells)
    return (grad_field, grad_spec, dw_in * grad_scale, dw_out * grad_scale)


def solution(mesh):
    placed = (
        P(("rep", "gx"), None, None, None),
        P(("rep", "gx"), None, None, None),
        P("gx", None, None),
        P(),
        P(),
    )
    return jax.shard_map(
        body,
        mesh=mesh,
        in_specs=placed,
        out_specs=(
            P(("rep", "gx"), None, None, None),
            P(("rep", "gx"), None, None),
            P("rep", None),
            P("rep", None),
        ),
        check_vma=False,
    )
```

```python
import functools
import math

import jax
import jax.numpy as jnp
import ml_dtypes
import numpy as np
from jax import lax
from jax.experimental import pallas as pl
from jax.experimental.pallas import tpu as pltpu
from jax.sharding import PartitionSpec as P

KZ = 16
KX = 16
GROUP = 8
LANES = 128
F32 = jnp.float32
BF16 = jnp.bfloat16
PHASES = 10


def make_tables(length_x, length_z):
    z_pos = np.arange(length_z)
    k_z = np.arange(KZ)
    angle_z = 2.0 * math.pi * (k_z[:, None] * z_pos[None, :] % length_z) / length_z
    cos_z, sin_z = np.cos(angle_z), np.sin(angle_z)
    k_weight = np.where(k_z == 0, 1.0, 2.0)[:, None]
    forward_z = np.concatenate([cos_z, -sin_z], 0) / math.sqrt(length_z)
    inverse_z = np.concatenate([k_weight * cos_z, -k_weight * sin_z], 0) / math.sqrt(length_z)
    j_index = np.arange(KX)
    k_x = np.where(j_index < KX // 2, j_index, length_x - KX + j_index)
    x_pos = np.arange(length_x)
    angle_x = 2.0 * math.pi * (k_x[:, None] * x_pos[None, :] % length_x) / length_x
    cosine_x = np.cos(angle_x) / math.sqrt(length_x)
    sine_x = np.sin(angle_x) / math.sqrt(length_x)
    eye = np.eye(KZ)
    kron_c, kron_s = np.kron(cosine_x, eye), np.kron(sine_x, eye)
    forward_x = np.concatenate([kron_c, kron_s], 0)
    inverse_x = np.concatenate([kron_c.T, kron_s.T], 0)

    def low(table):
        return table.astype(np.float32).astype(ml_dtypes.bfloat16)

    return low(forward_z), low(inverse_z), low(forward_x), low(inverse_x)


def gelu_parts(x):
    k = math.sqrt(2.0 / math.pi)
    sq = x * x
    t = jnp.tanh(k * x * (1.0 + 0.044715 * sq))
    half = 0.5 * (1.0 + t)
    slope = half + 0.5 * x * (1.0 - t * t) * (k * (1.0 + 3 * 0.044715 * sq))
    return x * half, slope


def dot(a, b, dims=((1,), (0,))):
    return lax.dot_general(a, b, (dims, ((), ())), preferred_element_type=F32)


NT = ((1,), (1,))
TN = ((0,), (0,))


def loop(low, high, step):
    if high - low <= 4:
        for i in range(low, high):
            step(i)
    else:
        lax.fori_loop(low, high, lambda i, c: (step(i), c)[1], 0)


def kernel(
    n, planes, rows, own, scale,
    field, cot, weight, w_in, w_out, fz, gz, tx, ti,
    out_field, out_spec, out_win, out_wout,
    s1, r1, s4, r4, s5, r5, s8, r8,
    s2, r2, s3, r3, s6, r6, s7, r7,
    sw, rw, sg, rg,
    wfull, xs, ys, ds, act, slope, branch, dw,
    send_sem, recv_sem,
):
    me = lax.axis_index("gx")
    low_lane = lax.broadcasted_iota(jnp.int32, (KZ, LANES), 1) < LANES // 2
    chans = LANES // 2
    per_x = rows // GROUP
    groups = planes * per_x

    barrier = pltpu.get_barrier_semaphore()

    def greet(i, c):
        pl.semaphore_signal(barrier, inc=1, device_id={"gx": lax.rem(me + i, n)})
        return c

    lax.fori_loop(1, n, greet, 0)

    def send(phase, src, dst):
        def one(i, c):
            to = lax.rem(me + i, n)
            pltpu.make_async_remote_copy(
                src_ref=src(to), dst_ref=dst.at[me],
                send_sem=send_sem.at[phase], recv_sem=recv_sem.at[phase],
                device_id={"gx": to},
            ).start()
            return c

        lax.fori_loop(1, n, one, 0)

    def exchange(phase, src, dst):
        send(phase, lambda to: src.at[to], dst)
        dst[me] = src[me]

    def bulk(phase, dst):
        some = dst.at[pl.ds(0, n - 1)]
        return pltpu.make_async_remote_copy(
            src_ref=some, dst_ref=some,
            send_sem=send_sem.at[phase], recv_sem=recv_sem.at[phase],
            device_id={"gx": lax.rem(me + 1, n)},
        )

    def swap(v):
        return pltpu.roll(v, LANES // 2, 1)

    def rotated(v, first):
        lane = lax.broadcasted_iota(jnp.int32, v.shape, 1) < LANES // 2
        turned = swap(v)
        return jnp.where(lane, first * turned, -first * turned)

    def place(g):
        return g // per_x, lax.rem(g, per_x) * GROUP if not isinstance(g, int) else (g % per_x) * GROUP

    def z_forward(g, slabs, table, dst):
        res = dot(table[...], slabs, NT)
        x, y0 = place(g)
        for b in range(GROUP // 2):
            real = res[:KZ, b * LANES:(b + 1) * LANES]
            imag = res[KZ:, b * LANES:(b + 1) * LANES]
            dst[y0 + 2 * b, x] = jnp.where(low_lane, real, swap(imag)).astype(BF16)
            dst[y0 + 2 * b + 1, x] = jnp.where(low_lane, swap(real), imag).astype(BF16)

    def z_inverse(g, src, table):
        x, y0 = place(g)
        pieces = []
        for b in range(GROUP // 2):
            even = src[y0 + 2 * b, x].astype(F32)
            odd = src[y0 + 2 * b + 1, x].astype(F32)
            pieces.append(jnp.concatenate(
                [jnp.where(low_lane, even, swap(odd)), jnp.where(low_lane, swap(even), odd)], 0))
        return dot(jnp.concatenate(pieces, 1).astype(BF16), table[...], TN)

    def x_forward(src, dst):
        data = src[...].reshape(n * planes * KZ, LANES)
        both = dot(tx[...], data)
        half = KX * KZ
        spec = both[:half] + rotated(both[half:], 1.0)
        for d in range(n):
            dst[d] = spec[d * own:(d + 1) * own].astype(dst.dtype)

    def x_inverse(src, dst):
        data = jnp.concatenate([src[d].astype(F32) for d in range(n)], 0).astype(BF16)
        both = dot(ti[...], data)
        half = n * planes * KZ
        res = both[:half] + rotated(both[half:], -1.0)
        dst[...] = res.astype(BF16).reshape(dst.shape)

    def spread(src, dst):
        for d in range(n):
            dst[d * own:(d + 1) * own, :] = src[d].astype(F32)

    def collect(src, dst):
        for d in range(n):
            dst[d] = src[d * own:(d + 1) * own, :].astype(dst.dtype)

    def to_lane(v):
        return jnp.concatenate([v[i * chans:(i + 1) * chans] for i in range(GROUP)], 1)

    def to_row(v):
        return jnp.concatenate([v[:, i * LANES:(i + 1) * LANES] for i in range(GROUP)], 0)

    def slab_rows(ref, g):
        return ref[pl.ds(g * GROUP, GROUP)].reshape(GROUP * chans, LANES)

    def network(g):
        u = to_lane(slab_rows(field, g))
        value, grad = gelu_parts(dot(w_in[...], u, TN))
        value = value.astype(BF16)
        act[g] = value
        slope[g] = grad.astype(BF16)
        branch[g] = to_row(dot(w_out[...], value, TN))

    def network_part(i):
        loop(i * groups // 4, (i + 1) * groups // 4, network)

    loop(0, groups, lambda g: z_forward(g, slab_rows(field, g), fz, s1))
    pl.semaphore_wait(barrier, n - 1)
    exchange(0, s1, r1)
    for m in range(own):
        w = weight[m].astype(F32)
        wfull[m] = jnp.concatenate([w, rotated(w, -1.0)], 0).astype(BF16)
    network_part(0)
    bulk(0, r1).wait_recv()
    x_forward(r1, s2)
    exchange(1, s2, r2)
    network_part(1)
    bulk(1, r2).wait_recv()
    spread(r2, xs)
    for m in range(own):
        at = pl.ds(m, n, stride=own)
        ys[at, :] = dot(xs[at, :].astype(BF16), wfull[m])
    collect(ys, s3)
    exchange(2, s3, r3)
    network_part(2)
    bulk(2, r3).wait_recv()
    x_inverse(r3, s4)
    exchange(3, s4, r4)
    network_part(3)
    bulk(3, r4).wait_recv()

    def point(g):
        pre = z_inverse(g, r4, gz) + branch[g]
        unused, grad = gelu_parts(pre)
        d_pre = (slab_rows(cot, g).astype(F32) * grad).astype(BF16)
        out_field[pl.ds(g * GROUP, GROUP)] = d_pre.reshape(GROUP, chans, LANES)
        z_forward(g, d_pre, gz, s5)

    loop(0, groups, point)
    exchange(4, s5, r5)
    dw[...] = jnp.zeros_like(dw)

    def network_back(g):
        d_pre = to_lane(slab_rows(out_field, g))
        d_act = (slope[g].astype(F32) * dot(w_out[...], d_pre)).astype(BF16)
        branch[g] = to_row(dot(w_in[...], d_act))
        u = to_lane(slab_rows(field, g))
        dw[:chans, :] += dot(u, d_act, NT)
        dw[chans:, :] += dot(d_pre, act[g], NT)

    loop(0, groups // 2, network_back)
    bulk(4, r5).wait_recv()
    x_forward(r5, s6)
    exchange(5, s6, r6)
    loop(groups // 2, groups, network_back)
    share = LANES // n
    for d in range(n):
        sw[d] = dw[d * share:(d + 1) * share, :]
    exchange(8, sw, rw)
    bulk(5, r6).wait_recv()
    spread(r6, ds)
    for m in range(own):
        at = pl.ds(m, n, stride=own)
        ys[at, :] = dot(ds[at, :].astype(BF16), wfull[m], NT)
    collect(ys, s7)
    exchange(6, s7, r7)
    for m in range(own):
        at = pl.ds(m, n, stride=own)
        full = dot(xs[at, :].astype(BF16), ds[at, :].astype(BF16), TN)
        out_spec[m] = full[:chans] + rotated(full[chans:], 1.0)
    bulk(8, rw).wait_recv()
    sg[0] = jnp.sum(rw[...], 0) * scale
    send(9, lambda to: sg.at[0], rg)
    rg[me] = sg[0]
    bulk(6, r7).wait_recv()
    x_inverse(r7, s8)
    exchange(7, s8, r8)
    bulk(9, rg).wait_recv()
    for d in range(n):
        dw[d * share:(d + 1) * share, :] = rg[d]
    out_win[...] = dw[:chans, :]
    out_wout[...] = dw[chans:, :].T
    bulk(7, r8).wait_recv()

    def finish(g):
        du = z_inverse(g, r8, fz) + branch[g]
        out_field[pl.ds(g * GROUP, GROUP)] = du.astype(BF16).reshape(GROUP, chans, LANES)

    loop(0, groups, finish)
    for phase, dst in enumerate((r1, r2, r3, r4, r5, r6, r7, r8, rw, rg)):
        bulk(phase, dst).wait_send()


def body(in_field, cotangent, spec_weight, w_in, w_out):
    n = lax.axis_size("gx")
    planes, rows, chans, z_cells = in_field.shape
    own = spec_weight.shape[0]
    length_x = planes * n
    assert rows == n and z_cells == LANES and 2 * chans == LANES
    fz, gz, tx, ti = make_tables(length_x, z_cells)
    slabs = planes * rows
    groups = slabs // GROUP
    hidden = w_in.shape[1]
    wire = BF16 if own % 16 == 0 else F32
    big = pltpu.VMEM((n, planes, KZ, LANES), BF16)
    small = pltpu.VMEM((n, own, LANES), wire)
    share = LANES // n
    scratch = [big] * 8 + [small] * 8 + [
        pltpu.VMEM((n, share, LANES), F32),
        pltpu.VMEM((n, share, LANES), F32),
        pltpu.VMEM((1, share, LANES), F32),
        pltpu.VMEM((n, share, LANES), F32),
        pltpu.VMEM((own, LANES, LANES), BF16),
        pltpu.VMEM((n * own, LANES), F32),
        pltpu.VMEM((n * own, LANES), F32),
        pltpu.VMEM((n * own, LANES), F32),
        pltpu.VMEM((groups, hidden, GROUP * LANES), BF16),
        pltpu.VMEM((groups, hidden, GROUP * LANES), BF16),
        pltpu.VMEM((groups, GROUP * chans, LANES), F32),
        pltpu.VMEM((LANES, LANES), F32),
        pltpu.SemaphoreType.DMA((PHASES,)),
        pltpu.SemaphoreType.DMA((PHASES,)),
    ]
    scale = 1.0 / math.sqrt(length_x * rows * z_cells)
    vmem = pl.BlockSpec(memory_space=pltpu.VMEM)
    grad_field, grad_spec, grad_w_in, grad_w_out = pl.pallas_call(
        functools.partial(kernel, n, planes, rows, own, scale),
        out_shape=(
            jax.ShapeDtypeStruct((slabs, chans, z_cells), BF16),
            jax.ShapeDtypeStruct(spec_weight.shape, F32),
            jax.ShapeDtypeStruct(w_in.shape, F32),
            jax.ShapeDtypeStruct(w_out.shape, F32),
        ),
        in_specs=[vmem] * 9,
        out_specs=(vmem,) * 4,
        scratch_shapes=scratch,
        compiler_params=pltpu.CompilerParams(
            collective_id=0, has_side_effects=True, vmem_limit_bytes=60 * 1024 * 1024
        ),
    )(
        in_field.reshape(slabs, chans, z_cells),
        cotangent.reshape(slabs, chans, z_cells),
        spec_weight, w_in, w_out,
        jnp.asarray(fz), jnp.asarray(gz), jnp.asarray(tx), jnp.asarray(ti),
    )
    return grad_field.reshape(in_field.shape), grad_spec, grad_w_in, grad_w_out


def solution(mesh):
    placed = (
        P(("rep", "gx"), None, None, None),
        P(("rep", "gx"), None, None, None),
        P("gx", None, None),
        P(),
        P(),
    )
    return jax.shard_map(
        body,
        mesh=mesh,
        in_specs=placed,
        out_specs=(
            P(("rep", "gx"), None, None, None),
            P(("rep", "gx"), None, None),
            P("rep", None),
            P("rep", None),
        ),
        check_vma=False,
    )
```

```python
import functools
import math

import jax
import jax.numpy as jnp
import ml_dtypes
import numpy as np
from jax import lax
from jax.experimental import pallas as pl
from jax.experimental.pallas import tpu as pltpu
from jax.sharding import PartitionSpec as P

KZ = 16
KX = 16
GROUP = 8
LANES = 128
F32 = jnp.float32
BF16 = jnp.bfloat16
PHASES = 10


def make_tables(length_x, length_z):
    z_pos = np.arange(length_z)
    k_z = np.arange(KZ)
    angle_z = 2.0 * math.pi * (k_z[:, None] * z_pos[None, :] % length_z) / length_z
    cos_z, sin_z = np.cos(angle_z), np.sin(angle_z)
    k_weight = np.where(k_z == 0, 1.0, 2.0)[:, None]
    forward_z = np.concatenate([cos_z, -sin_z], 0) / math.sqrt(length_z)
    inverse_z = np.concatenate([k_weight * cos_z, -k_weight * sin_z], 0) / math.sqrt(length_z)
    j_index = np.arange(KX)
    k_x = np.where(j_index < KX // 2, j_index, length_x - KX + j_index)
    x_pos = np.arange(length_x)
    angle_x = 2.0 * math.pi * (k_x[:, None] * x_pos[None, :] % length_x) / length_x
    cosine_x = np.cos(angle_x) / math.sqrt(length_x)
    sine_x = np.sin(angle_x) / math.sqrt(length_x)
    eye = np.eye(KZ)
    kron_c, kron_s = np.kron(cosine_x, eye), np.kron(sine_x, eye)
    forward_x = np.concatenate([kron_c, kron_s], 0)
    inverse_x = np.concatenate([kron_c.T, kron_s.T], 0)

    def low(table):
        return table.astype(np.float32).astype(ml_dtypes.bfloat16)

    return low(forward_z), low(inverse_z), low(forward_x), low(inverse_x)


def gelu_parts(x):
    k = math.sqrt(2.0 / math.pi)
    sq = x * x
    t = jnp.tanh(k * x * (1.0 + 0.044715 * sq))
    half = 0.5 * (1.0 + t)
    slope = half + 0.5 * x * (1.0 - t * t) * (k * (1.0 + 3 * 0.044715 * sq))
    return x * half, slope


def dot(a, b, dims=((1,), (0,))):
    return lax.dot_general(a, b, (dims, ((), ())), preferred_element_type=F32)


NT = ((1,), (1,))
TN = ((0,), (0,))


def slabs_of(src, table, x, y0):
    low_lane = lax.broadcasted_iota(jnp.int32, (KZ, LANES), 1) < LANES // 2
    pieces = []
    for b in range(GROUP // 2):
        even = src[y0 + 2 * b, x].astype(F32)
        odd = src[y0 + 2 * b + 1, x].astype(F32)
        real = jnp.where(low_lane, even, pltpu.roll(odd, LANES // 2, 1))
        imag = jnp.where(low_lane, pltpu.roll(even, LANES // 2, 1), odd)
        pieces.append(jnp.concatenate([real, imag], 0))
    return dot(jnp.concatenate(pieces, 1).astype(BF16), table[...], TN)


def loop(low, high, step):
    if high - low <= 4:
        for i in range(low, high):
            step(i)
    else:
        lax.fori_loop(low, high, lambda i, c: (step(i), c)[1], 0)


def kernel(
    n, planes, rows, own, scale,
    field_hbm, cot_hbm, weight_hbm, tx_hbm, ti_hbm, w_in, w_out_t, fz, gz,
    out_field, out_spec, out_dw, out_coeffs,
    s1, r1, s4, r4, s5, r5, s8, r8,
    s2, r2, s3, r3, s6, r6, s7, r7,
    sw, rw, sg, rg,
    wfull, xs, ys, ds, act, slope, branch, dw,
    field, cot, weight, tx, ti,
    send_sem, recv_sem, load_sem,
):
    me = lax.axis_index("gx")
    loads = [
        pltpu.make_async_copy(src, dst, load_sem.at[i])
        for i, (src, dst) in enumerate((
            (field_hbm, field), (weight_hbm, weight), (tx_hbm, tx), (ti_hbm, ti), (cot_hbm, cot)))
    ]
    for load in loads:
        load.start()
    low_lane = lax.broadcasted_iota(jnp.int32, (KZ, LANES), 1) < LANES // 2
    chans = LANES // 2
    per_x = rows // GROUP
    groups = planes * per_x

    barrier = pltpu.get_barrier_semaphore()

    def greet(i, c):
        pl.semaphore_signal(barrier, inc=1, device_id={"gx": lax.rem(me + i, n)})
        return c

    lax.fori_loop(1, n, greet, 0)

    def send(phase, src, dst):
        def one(i, c):
            to = lax.rem(me + i, n)
            pltpu.make_async_remote_copy(
                src_ref=src(to), dst_ref=dst.at[me],
                send_sem=send_sem.at[phase], recv_sem=recv_sem.at[phase],
                device_id={"gx": to},
            ).start()
            return c

        lax.fori_loop(1, n, one, 0)

    def exchange(phase, src, dst):
        send(phase, lambda to: src.at[to], dst)
        dst[me] = src[me]

    def bulk(phase, dst):
        some = dst.at[pl.ds(0, n - 1)]
        return pltpu.make_async_remote_copy(
            src_ref=some, dst_ref=some,
            send_sem=send_sem.at[phase], recv_sem=recv_sem.at[phase],
            device_id={"gx": lax.rem(me + 1, n)},
        )

    def swap(v):
        return pltpu.roll(v, LANES // 2, 1)

    def rotated(v, first):
        lane = lax.broadcasted_iota(jnp.int32, v.shape, 1) < LANES // 2
        turned = swap(v)
        return jnp.where(lane, first * turned, -first * turned)

    def place(g):
        return g // per_x, lax.rem(g, per_x) * GROUP if not isinstance(g, int) else (g % per_x) * GROUP

    def z_forward(g, slabs, table, dst):
        res = dot(table[...], slabs, NT)
        x, y0 = place(g)
        for b in range(GROUP // 2):
            real = res[:KZ, b * LANES:(b + 1) * LANES]
            imag = res[KZ:, b * LANES:(b + 1) * LANES]
            dst[y0 + 2 * b, x] = jnp.where(low_lane, real, swap(imag)).astype(BF16)
            dst[y0 + 2 * b + 1, x] = jnp.where(low_lane, swap(real), imag).astype(BF16)

    def z_inverse(g, src, table):
        return slabs_of(src, table, *place(g))

    def x_forward(src, dst):
        data = src[...].reshape(n * planes * KZ, LANES)
        both = dot(tx[...], data)
        half = KX * KZ
        spec = both[:half] + rotated(both[half:], 1.0)
        for d in range(n):
            dst[d] = spec[d * own:(d + 1) * own].astype(dst.dtype)

    def x_inverse(src, dst):
        data = jnp.concatenate([src[d].astype(F32) for d in range(n)], 0).astype(BF16)
        both = dot(ti[...], data)
        half = n * planes * KZ
        res = both[:half] + rotated(both[half:], -1.0)
        dst[...] = res.astype(BF16).reshape(dst.shape)

    def spread(src, dst):
        for d in range(n):
            dst[d * own:(d + 1) * own, :] = src[d].astype(F32)

    def collect(src, dst):
        for d in range(n):
            dst[d] = src[d * own:(d + 1) * own, :].astype(dst.dtype)

    def to_lane(v):
        return jnp.concatenate([v[i * chans:(i + 1) * chans] for i in range(GROUP)], 1)

    def to_row(v):
        return jnp.concatenate([v[:, i * LANES:(i + 1) * LANES] for i in range(GROUP)], 0)

    def slab_rows(ref, g):
        return ref[pl.ds(g * GROUP, GROUP)].reshape(GROUP * chans, LANES)

    def network(g):
        u = to_lane(slab_rows(field, g))
        value, grad = gelu_parts(dot(w_in[...], u, TN))
        value = value.astype(BF16)
        act[g] = value
        slope[g] = grad.astype(BF16)
        branch[g] = to_row(dot(w_out_t[...], value))

    def network_part(i):
        loop(i * groups // 4, (i + 1) * groups // 4, network)

    loads[0].wait()
    loop(0, groups, lambda g: z_forward(g, slab_rows(field, g), fz, s1))
    pl.semaphore_wait(barrier, n - 1)
    exchange(0, s1, r1)
    loads[1].wait()
    for m in range(own):
        w = weight[m].astype(F32)
        wfull[m] = jnp.concatenate([w, rotated(w, -1.0)], 0).astype(BF16)
    network_part(0)
    for load in loads[2:]:
        load.wait()
    bulk(0, r1).wait_recv()
    x_forward(r1, s2)
    exchange(1, s2, r2)
    network_part(1)
    bulk(1, r2).wait_recv()
    spread(r2, xs)
    for m in range(own):
        at = pl.ds(m, n, stride=own)
        ys[at, :] = dot(xs[at, :].astype(BF16), wfull[m])
    collect(ys, s3)
    exchange(2, s3, r3)
    network_part(2)
    bulk(2, r3).wait_recv()
    x_inverse(r3, s4)
    exchange(3, s4, r4)
    network_part(3)
    bulk(3, r4).wait_recv()

    def point(g):
        pre = z_inverse(g, r4, gz) + branch[g]
        unused, grad = gelu_parts(pre)
        d_pre = (slab_rows(cot, g).astype(F32) * grad).astype(BF16)
        out_field[pl.ds(g * GROUP, GROUP)] = d_pre.reshape(GROUP, chans, LANES)
        z_forward(g, d_pre, gz, s5)

    loop(0, groups, point)
    exchange(4, s5, r5)
    dw[...] = jnp.zeros_like(dw)

    def network_back(g):
        d_pre = to_lane(slab_rows(out_field, g))
        d_act = (slope[g].astype(F32) * dot(w_out_t[...], d_pre, TN)).astype(BF16)
        du = to_row(dot(w_in[...], d_act))
        out_field[pl.ds(g * GROUP, GROUP)] = du.astype(BF16).reshape(GROUP, chans, LANES)
        u = to_lane(slab_rows(field, g))
        dw[:chans, :] += dot(u, d_act, NT)
        dw[chans:, :] += dot(d_pre, act[g], NT)

    loop(0, groups // 2, network_back)
    bulk(4, r5).wait_recv()
    x_forward(r5, s6)
    exchange(5, s6, r6)
    loop(groups // 2, groups, network_back)
    share = LANES // n
    for d in range(n):
        sw[d] = dw[d * share:(d + 1) * share, :]
    exchange(8, sw, rw)
    bulk(5, r6).wait_recv()
    spread(r6, ds)
    for m in range(own):
        at = pl.ds(m, n, stride=own)
        ys[at, :] = dot(ds[at, :].astype(BF16), wfull[m], NT)
    collect(ys, s7)
    exchange(6, s7, r7)
    for m in range(own):
        at = pl.ds(m, n, stride=own)
        full = dot(xs[at, :].astype(BF16), ds[at, :].astype(BF16), TN)
        out_spec[m] = full[:chans] + rotated(full[chans:], 1.0)
    bulk(8, rw).wait_recv()
    sg[0] = jnp.sum(rw[...], 0) * scale
    send(9, lambda to: sg.at[0], rg)
    rg[me] = sg[0]
    bulk(6, r7).wait_recv()
    x_inverse(r7, s8)
    exchange(7, s8, r8)
    bulk(9, rg).wait_recv()
    for d in range(n):
        out_dw[d * share:(d + 1) * share, :] = rg[d]
    bulk(7, r8).wait_recv()
    out_coeffs[...] = r8[...]
    for phase, dst in enumerate((r1, r2, r3, r4, r5, r6, r7, r8, rw, rg)):
        bulk(phase, dst).wait_send()


def finish_kernel(
    planes, rows, coeffs, network, spec, dw, fz, out_field, out_spec, out_win, out_wout_t, sems
):
    chans = LANES // 2
    per_x = rows // GROUP
    copies = [
        pltpu.make_async_copy(spec, out_spec, sems.at[0]),
        pltpu.make_async_copy(dw.at[pl.ds(0, chans)], out_win, sems.at[1]),
        pltpu.make_async_copy(dw.at[pl.ds(chans, chans)], out_wout_t, sems.at[2]),
    ]
    for copy in copies:
        copy.start()

    def finish(g):
        x, y0 = g // per_x, (g % per_x if isinstance(g, int) else lax.rem(g, per_x)) * GROUP
        at = pl.ds(g * GROUP, GROUP)
        du = slabs_of(coeffs, fz, x, y0) + network[at].reshape(GROUP * chans, LANES).astype(F32)
        out_field[at] = du.astype(BF16).reshape(GROUP, chans, LANES)

    loop(0, planes * per_x, finish)
    for copy in copies:
        copy.wait()


def body(in_field, cotangent, spec_weight, w_in, w_out):
    n = lax.axis_size("gx")
    planes, rows, chans, z_cells = in_field.shape
    own = spec_weight.shape[0]
    length_x = planes * n
    assert rows == n and z_cells == LANES and 2 * chans == LANES
    fz, gz, tx, ti = make_tables(length_x, z_cells)
    slabs = planes * rows
    groups = slabs // GROUP
    hidden = w_in.shape[1]
    wire = BF16 if own % 16 == 0 else F32
    big = pltpu.VMEM((n, planes, KZ, LANES), BF16)
    small = pltpu.VMEM((n, own, LANES), wire)
    share = LANES // n
    scratch = [big] * 8 + [small] * 8 + [
        pltpu.VMEM((n, share, LANES), F32),
        pltpu.VMEM((n, share, LANES), F32),
        pltpu.VMEM((1, share, LANES), F32),
        pltpu.VMEM((n, share, LANES), F32),
        pltpu.VMEM((own, LANES, LANES), BF16),
        pltpu.VMEM((n * own, LANES), F32),
        pltpu.VMEM((n * own, LANES), F32),
        pltpu.VMEM((n * own, LANES), F32),
        pltpu.VMEM((groups, hidden, GROUP * LANES), BF16),
        pltpu.VMEM((groups, hidden, GROUP * LANES), BF16),
        pltpu.VMEM((groups, GROUP * chans, LANES), F32),
        pltpu.VMEM((LANES, LANES), F32),
        pltpu.VMEM((slabs, chans, z_cells), BF16),
        pltpu.VMEM((slabs, chans, z_cells), BF16),
        pltpu.VMEM(spec_weight.shape, BF16),
        pltpu.VMEM(tx.shape, BF16),
        pltpu.VMEM(ti.shape, BF16),
        pltpu.SemaphoreType.DMA((PHASES,)),
        pltpu.SemaphoreType.DMA((PHASES,)),
        pltpu.SemaphoreType.DMA((5,)),
    ]
    scale = 1.0 / math.sqrt(length_x * rows * z_cells)
    vmem = pl.BlockSpec(memory_space=pltpu.VMEM)
    hbm = pl.BlockSpec(memory_space=pl.ANY)
    field_shape = jax.ShapeDtypeStruct((slabs, chans, z_cells), BF16)
    spec_shape = jax.ShapeDtypeStruct(spec_weight.shape, F32)
    fz, gz = jnp.asarray(fz), jnp.asarray(gz)
    network, spec, dw, coeffs = pl.pallas_call(
        functools.partial(kernel, n, planes, rows, own, scale),
        out_shape=(
            field_shape,
            spec_shape,
            jax.ShapeDtypeStruct((LANES, LANES), F32),
            jax.ShapeDtypeStruct((n, planes, KZ, LANES), BF16),
        ),
        in_specs=[hbm] * 5 + [vmem] * 4,
        out_specs=(vmem,) * 4,
        scratch_shapes=scratch,
        compiler_params=pltpu.CompilerParams(
            collective_id=0, has_side_effects=True, vmem_limit_bytes=60 * 1024 * 1024
        ),
    )(
        in_field.reshape(slabs, chans, z_cells),
        cotangent.reshape(slabs, chans, z_cells),
        spec_weight, jnp.asarray(tx), jnp.asarray(ti), w_in, w_out.T, fz, gz,
    )
    grad_field, grad_spec, grad_w_in, grad_w_out_t = pl.pallas_call(
        functools.partial(finish_kernel, planes, rows),
        out_shape=(
            field_shape,
            spec_shape,
            jax.ShapeDtypeStruct(w_in.shape, F32),
            jax.ShapeDtypeStruct(w_out.shape[::-1], F32),
        ),
        in_specs=[vmem, vmem, hbm, hbm, vmem],
        out_specs=(vmem, hbm, hbm, hbm),
        scratch_shapes=[pltpu.SemaphoreType.DMA((3,))],
        compiler_params=pltpu.CompilerParams(vmem_limit_bytes=32 * 1024 * 1024),
    )(coeffs, network, spec, dw, fz)
    return grad_field.reshape(in_field.shape), grad_spec, grad_w_in, grad_w_out_t.T


def solution(mesh):
    placed = (
        P(("rep", "gx"), None, None, None),
        P(("rep", "gx"), None, None, None),
        P("gx", None, None),
        P(),
        P(),
    )
    return jax.shard_map(
        body,
        mesh=mesh,
        in_specs=placed,
        out_specs=(
            P(("rep", "gx"), None, None, None),
            P(("rep", "gx"), None, None),
            P("rep", None),
            P("rep", None),
        ),
        check_vma=False,
    )
```

```python
import functools
import math

import jax
import jax.numpy as jnp
import ml_dtypes
import numpy as np
from jax import lax
from jax.experimental import pallas as pl
from jax.experimental.pallas import tpu as pltpu
from jax.sharding import PartitionSpec as P

KZ = 16
KX = 16
GROUP = 8
LANES = 128
F32 = jnp.float32
BF16 = jnp.bfloat16
PHASES = 10


def make_tables(length_x, length_z):
    z_pos = np.arange(length_z)
    k_z = np.arange(KZ)
    angle_z = 2.0 * math.pi * (k_z[:, None] * z_pos[None, :] % length_z) / length_z
    cos_z, sin_z = np.cos(angle_z), np.sin(angle_z)
    k_weight = np.where(k_z == 0, 1.0, 2.0)[:, None]
    forward_z = np.concatenate([cos_z, -sin_z], 0) / math.sqrt(length_z)
    inverse_z = np.concatenate([k_weight * cos_z, -k_weight * sin_z], 0) / math.sqrt(length_z)
    j_index = np.arange(KX)
    k_x = np.where(j_index < KX // 2, j_index, length_x - KX + j_index)
    x_pos = np.arange(length_x)
    angle_x = 2.0 * math.pi * (k_x[:, None] * x_pos[None, :] % length_x) / length_x
    cosine_x = np.cos(angle_x) / math.sqrt(length_x)
    sine_x = np.sin(angle_x) / math.sqrt(length_x)
    eye = np.eye(KZ)
    kron_c, kron_s = np.kron(cosine_x, eye), np.kron(sine_x, eye)
    forward_x = np.concatenate([kron_c, kron_s], 0)
    inverse_x = np.concatenate([kron_c.T, kron_s.T], 0)

    def low(table):
        return table.astype(np.float32).astype(ml_dtypes.bfloat16)

    return low(forward_z), low(inverse_z), low(forward_x), low(inverse_x)


def gelu_parts(x):
    k = math.sqrt(2.0 / math.pi)
    sq = x * x
    t = jnp.tanh(k * x * (1.0 + 0.044715 * sq))
    half = 0.5 * (1.0 + t)
    slope = half + 0.5 * x * (1.0 - t * t) * (k * (1.0 + 3 * 0.044715 * sq))
    return x * half, slope


def dot(a, b, dims=((1,), (0,))):
    return lax.dot_general(a, b, (dims, ((), ())), preferred_element_type=F32)


NT = ((1,), (1,))
TN = ((0,), (0,))


def slabs_of(src, table, x, y0):
    low_lane = lax.broadcasted_iota(jnp.int32, (KZ, LANES), 1) < LANES // 2
    pieces = []
    for b in range(GROUP // 2):
        even = src[y0 + 2 * b, x].astype(F32)
        odd = src[y0 + 2 * b + 1, x].astype(F32)
        real = jnp.where(low_lane, even, pltpu.roll(odd, LANES // 2, 1))
        imag = jnp.where(low_lane, pltpu.roll(even, LANES // 2, 1), odd)
        pieces.append(jnp.concatenate([real, imag], 0))
    return dot(jnp.concatenate(pieces, 1).astype(BF16), table[...], TN)


def loop(low, high, step):
    if high - low <= 4:
        for i in range(low, high):
            step(i)
    else:
        lax.fori_loop(low, high, lambda i, c: (step(i), c)[1], 0)


def kernel(
    n, planes, rows, own, scale,
    field_hbm, cot_hbm, weight_hbm, tx_hbm, ti_hbm, w_in, w_out_t, fz, gz,
    out_field, out_spec, out_dw, out_coeffs,
    s1, r1, s4, r4, s5, r5, s8, r8,
    s2, r2, s3, r3, s6, r6, s7, r7,
    sw, rw, sg, rg,
    wfull, xs, ys, ds, act, slope, branch, dw,
    field, cot, weight, tx, ti,
    send_sem, recv_sem, load_sem,
):
    me = lax.axis_index("gx")
    loads = [
        pltpu.make_async_copy(src, dst, load_sem.at[i])
        for i, (src, dst) in enumerate((
            (field_hbm, field), (weight_hbm, weight), (tx_hbm, tx), (ti_hbm, ti), (cot_hbm, cot)))
    ]
    for load in loads:
        load.start()
    low_lane = lax.broadcasted_iota(jnp.int32, (KZ, LANES), 1) < LANES // 2
    chans = LANES // 2
    per_x = rows // GROUP
    groups = planes * per_x

    barrier = pltpu.get_barrier_semaphore()

    def greet(i, c):
        pl.semaphore_signal(barrier, inc=1, device_id={"gx": lax.rem(me + i, n)})
        return c

    lax.fori_loop(1, n, greet, 0)

    def send(phase, src, dst):
        def one(i, c):
            to = lax.rem(me + i, n)
            pltpu.make_async_remote_copy(
                src_ref=src(to), dst_ref=dst.at[me],
                send_sem=send_sem.at[phase], recv_sem=recv_sem.at[phase],
                device_id={"gx": to},
            ).start()
            return c

        lax.fori_loop(1, n, one, 0)

    def exchange(phase, src, dst):
        send(phase, lambda to: src.at[to], dst)
        dst[me] = src[me]

    def bulk(phase, dst):
        some = dst.at[pl.ds(0, n - 1)]
        return pltpu.make_async_remote_copy(
            src_ref=some, dst_ref=some,
            send_sem=send_sem.at[phase], recv_sem=recv_sem.at[phase],
            device_id={"gx": lax.rem(me + 1, n)},
        )

    def swap(v):
        return pltpu.roll(v, LANES // 2, 1)

    def rotated(v, first):
        lane = lax.broadcasted_iota(jnp.int32, v.shape, 1) < LANES // 2
        turned = swap(v)
        return jnp.where(lane, first * turned, -first * turned)

    def place(g):
        return g // per_x, lax.rem(g, per_x) * GROUP if not isinstance(g, int) else (g % per_x) * GROUP

    def z_forward(g, slabs, table, dst):
        res = dot(table[...], slabs, NT)
        x, y0 = place(g)
        for b in range(GROUP // 2):
            real = res[:KZ, b * LANES:(b + 1) * LANES]
            imag = res[KZ:, b * LANES:(b + 1) * LANES]
            dst[y0 + 2 * b, x] = jnp.where(low_lane, real, swap(imag)).astype(BF16)
            dst[y0 + 2 * b + 1, x] = jnp.where(low_lane, swap(real), imag).astype(BF16)

    def z_inverse(g, src, table):
        return slabs_of(src, table, *place(g))

    def x_forward(src, dst):
        data = src[...].reshape(n * planes * KZ, LANES)
        both = dot(tx[...], data)
        half = KX * KZ
        spec = both[:half] + rotated(both[half:], 1.0)
        for d in range(n):
            dst[d] = spec[d * own:(d + 1) * own].astype(dst.dtype)

    def x_inverse(src, dst):
        data = jnp.concatenate([src[d].astype(F32) for d in range(n)], 0).astype(BF16)
        both = dot(ti[...], data)
        half = n * planes * KZ
        res = both[:half] + rotated(both[half:], -1.0)
        dst[...] = res.astype(BF16).reshape(dst.shape)

    def spread(src, dst):
        for d in range(n):
            dst[d * own:(d + 1) * own, :] = src[d].astype(F32)

    def collect(src, dst):
        for d in range(n):
            dst[d] = src[d * own:(d + 1) * own, :].astype(dst.dtype)

    def to_lane(v):
        return jnp.concatenate([v[i * chans:(i + 1) * chans] for i in range(GROUP)], 1)

    def to_row(v):
        return jnp.concatenate([v[:, i * LANES:(i + 1) * LANES] for i in range(GROUP)], 0)

    def slab_rows(ref, g):
        return ref[pl.ds(g * GROUP, GROUP)].reshape(GROUP * chans, LANES)

    def network(g):
        u = to_lane(slab_rows(field, g))
        value, grad = gelu_parts(dot(w_in[...], u, TN))
        value = value.astype(BF16)
        act[g] = value
        slope[g] = grad.astype(BF16)
        branch[g] = to_row(dot(w_out_t[...], value))

    def network_part(i):
        loop(i * groups // 4, (i + 1) * groups // 4, network)

    loads[0].wait()
    loop(0, groups, lambda g: z_forward(g, slab_rows(field, g), fz, s1))
    pl.semaphore_wait(barrier, n - 1)
    exchange(0, s1, r1)
    loads[1].wait()
    for m in range(own):
        w = weight[m].astype(F32)
        wfull[m] = jnp.concatenate([w, rotated(w, -1.0)], 0).astype(BF16)
    network_part(0)
    for load in loads[2:]:
        load.wait()
    bulk(0, r1).wait_recv()
    x_forward(r1, s2)
    exchange(1, s2, r2)
    network_part(1)
    bulk(1, r2).wait_recv()
    spread(r2, xs)
    for m in range(own):
        at = pl.ds(m, n, stride=own)
        ys[at, :] = dot(xs[at, :].astype(BF16), wfull[m])
    collect(ys, s3)
    exchange(2, s3, r3)
    network_part(2)
    bulk(2, r3).wait_recv()
    x_inverse(r3, s4)
    exchange(3, s4, r4)
    network_part(3)
    bulk(3, r4).wait_recv()

    def point(g):
        pre = z_inverse(g, r4, gz) + branch[g]
        unused, grad = gelu_parts(pre)
        d_pre = (slab_rows(cot, g).astype(F32) * grad).astype(BF16)
        out_field[pl.ds(g * GROUP, GROUP)] = d_pre.reshape(GROUP, chans, LANES)
        z_forward(g, d_pre, gz, s5)

    loop(0, groups, point)
    exchange(4, s5, r5)
    dw[...] = jnp.zeros_like(dw)

    def network_back(g):
        d_pre = to_lane(slab_rows(out_field, g))
        d_act = (slope[g].astype(F32) * dot(w_out_t[...], d_pre, TN)).astype(BF16)
        du = to_row(dot(w_in[...], d_act))
        out_field[pl.ds(g * GROUP, GROUP)] = du.astype(BF16).reshape(GROUP, chans, LANES)
        u = to_lane(slab_rows(field, g))
        dw[:chans, :] += dot(u, d_act, NT)
        dw[chans:, :] += dot(d_pre, act[g], NT)

    loop(0, groups // 2, network_back)
    bulk(4, r5).wait_recv()
    x_forward(r5, s6)
    exchange(5, s6, r6)
    loop(groups // 2, groups, network_back)
    share = LANES // n
    for d in range(n):
        sw[d] = dw[d * share:(d + 1) * share, :]
    exchange(8, sw, rw)
    bulk(5, r6).wait_recv()
    spread(r6, ds)
    for m in range(own):
        at = pl.ds(m, n, stride=own)
        ys[at, :] = dot(ds[at, :].astype(BF16), wfull[m], NT)
    collect(ys, s7)
    exchange(6, s7, r7)
    for m in range(own):
        at = pl.ds(m, n, stride=own)
        full = dot(xs[at, :].astype(BF16), ds[at, :].astype(BF16), TN)
        out_spec[m] = full[:chans] + rotated(full[chans:], 1.0)
    bulk(8, rw).wait_recv()
    sg[0] = jnp.sum(rw[...], 0) * scale
    send(9, lambda to: sg.at[0], rg)
    rg[me] = sg[0]
    bulk(6, r7).wait_recv()
    x_inverse(r7, s8)
    exchange(7, s8, r8)
    bulk(9, rg).wait_recv()
    for d in range(n):
        out_dw[d * share:(d + 1) * share, :] = rg[d]
    bulk(7, r8).wait_recv()
    out_coeffs[...] = r8[...]
    for phase, dst in enumerate((r1, r2, r3, r4, r5, r6, r7, r8, rw, rg)):
        bulk(phase, dst).wait_send()


def finish_kernel(
    planes, rows, coeffs, network, spec, dw, fz, out_field, out_spec, out_win, out_wout_t, sems
):
    chans = LANES // 2
    per_x = rows // GROUP
    copies = [
        pltpu.make_async_copy(spec, out_spec, sems.at[0]),
        pltpu.make_async_copy(dw.at[pl.ds(0, chans)], out_win, sems.at[1]),
        pltpu.make_async_copy(dw.at[pl.ds(chans, chans)], out_wout_t, sems.at[2]),
    ]
    for copy in copies:
        copy.start()

    def finish(g):
        x, y0 = g // per_x, (g % per_x if isinstance(g, int) else lax.rem(g, per_x)) * GROUP
        at = pl.ds(g * GROUP, GROUP)
        du = slabs_of(coeffs, fz, x, y0) + network[at].reshape(GROUP * chans, LANES).astype(F32)
        out_field[at] = du.astype(BF16).reshape(GROUP, chans, LANES)

    loop(0, planes * per_x, finish)
    for copy in copies:
        copy.wait()


def body(in_field, cotangent, spec_weight, w_in, w_out):
    n = lax.axis_size("gx")
    planes, rows, chans, z_cells = in_field.shape
    own = spec_weight.shape[0]
    length_x = planes * n
    assert rows == n and z_cells == LANES and 2 * chans == LANES
    fz, gz, tx, ti = make_tables(length_x, z_cells)
    slabs = planes * rows
    groups = slabs // GROUP
    hidden = w_in.shape[1]
    wire = BF16 if own % 16 == 0 else F32
    big = pltpu.VMEM((n, planes, KZ, LANES), BF16)
    small = pltpu.VMEM((n, own, LANES), wire)
    share = LANES // n
    scratch = [big] * 8 + [small] * 8 + [
        pltpu.VMEM((n, share, LANES), F32),
        pltpu.VMEM((n, share, LANES), F32),
        pltpu.VMEM((1, share, LANES), F32),
        pltpu.VMEM((n, share, LANES), F32),
        pltpu.VMEM((own, LANES, LANES), BF16),
        pltpu.VMEM((n * own, LANES), F32),
        pltpu.VMEM((n * own, LANES), F32),
        pltpu.VMEM((n * own, LANES), F32),
        pltpu.VMEM((groups, hidden, GROUP * LANES), BF16),
        pltpu.VMEM((groups, hidden, GROUP * LANES), BF16),
        pltpu.VMEM((groups, GROUP * chans, LANES), F32),
        pltpu.VMEM((LANES, LANES), F32),
        pltpu.VMEM((slabs, chans, z_cells), BF16),
        pltpu.VMEM((slabs, chans, z_cells), BF16),
        pltpu.VMEM(spec_weight.shape, BF16),
        pltpu.VMEM(tx.shape, BF16),
        pltpu.VMEM(ti.shape, BF16),
        pltpu.SemaphoreType.DMA((PHASES,)),
        pltpu.SemaphoreType.DMA((PHASES,)),
        pltpu.SemaphoreType.DMA((5,)),
    ]
    scale = 1.0 / math.sqrt(length_x * rows * z_cells)
    vmem = pl.BlockSpec(memory_space=pltpu.VMEM)
    hbm = pl.BlockSpec(memory_space=pl.ANY)
    field_shape = jax.ShapeDtypeStruct((slabs, chans, z_cells), BF16)
    spec_shape = jax.ShapeDtypeStruct(spec_weight.shape, F32)
    fz, gz = jnp.asarray(fz), jnp.asarray(gz)
    network, spec, dw, coeffs = pl.pallas_call(
        functools.partial(kernel, n, planes, rows, own, scale),
        out_shape=(
            field_shape,
            spec_shape,
            jax.ShapeDtypeStruct((LANES, LANES), F32),
            jax.ShapeDtypeStruct((n, planes, KZ, LANES), BF16),
        ),
        in_specs=[hbm] * 5 + [vmem] * 4,
        out_specs=(vmem,) * 4,
        scratch_shapes=scratch,
        compiler_params=pltpu.CompilerParams(
            collective_id=0, has_side_effects=True, vmem_limit_bytes=60 * 1024 * 1024
        ),
    )(
        in_field.reshape(slabs, chans, z_cells),
        cotangent.reshape(slabs, chans, z_cells),
        spec_weight, jnp.asarray(tx), jnp.asarray(ti), w_in, w_out.T, fz, gz,
    )
    grad_field, grad_spec, grad_w_in, grad_w_out_t = pl.pallas_call(
        functools.partial(finish_kernel, planes, rows),
        out_shape=(
            field_shape,
            spec_shape,
            jax.ShapeDtypeStruct(w_in.shape, F32),
            jax.ShapeDtypeStruct(w_out.shape[::-1], F32),
        ),
        in_specs=[vmem, vmem, hbm, hbm, vmem],
        out_specs=(vmem, hbm, hbm, hbm),
        scratch_shapes=[pltpu.SemaphoreType.DMA((3,))],
        compiler_params=pltpu.CompilerParams(vmem_limit_bytes=63 * 1024 * 1024),
    )(coeffs, network, spec, dw, fz)
    return grad_field.reshape(in_field.shape), grad_spec, grad_w_in, grad_w_out_t.T


def solution(mesh):
    placed = (
        P(("rep", "gx"), None, None, None),
        P(("rep", "gx"), None, None, None),
        P("gx", None, None),
        P(),
        P(),
    )
    return jax.shard_map(
        body,
        mesh=mesh,
        in_specs=placed,
        out_specs=(
            P(("rep", "gx"), None, None, None),
            P(("rep", "gx"), None, None),
            P("rep", None),
            P("rep", None),
        ),
        check_vma=False,
    )
```

```python
import functools
import math

import jax
import jax.numpy as jnp
import ml_dtypes
import numpy as np
from jax import lax
from jax.experimental import pallas as pl
from jax.experimental.pallas import tpu as pltpu
from jax.sharding import PartitionSpec as P

KZ = 16
KX = 16
GROUP = 8
LANES = 128
F32 = jnp.float32
BF16 = jnp.bfloat16
PHASES = 10


def make_tables(length_x, length_z):
    z_pos = np.arange(length_z)
    k_z = np.arange(KZ)
    angle_z = 2.0 * math.pi * (k_z[:, None] * z_pos[None, :] % length_z) / length_z
    cos_z, sin_z = np.cos(angle_z), np.sin(angle_z)
    k_weight = np.where(k_z == 0, 1.0, 2.0)[:, None]
    forward_z = np.concatenate([cos_z, -sin_z], 0) / math.sqrt(length_z)
    inverse_z = np.concatenate([k_weight * cos_z, -k_weight * sin_z], 0) / math.sqrt(length_z)
    j_index = np.arange(KX)
    k_x = np.where(j_index < KX // 2, j_index, length_x - KX + j_index)
    x_pos = np.arange(length_x)
    angle_x = 2.0 * math.pi * (k_x[:, None] * x_pos[None, :] % length_x) / length_x
    cosine_x = np.cos(angle_x) / math.sqrt(length_x)
    sine_x = np.sin(angle_x) / math.sqrt(length_x)
    eye = np.eye(KZ)
    kron_c, kron_s = np.kron(cosine_x, eye), np.kron(sine_x, eye)
    forward_x = np.concatenate([kron_c, kron_s], 0)
    inverse_x = np.concatenate([kron_c.T, kron_s.T], 0)

    def low(table):
        return table.astype(np.float32).astype(ml_dtypes.bfloat16)

    return low(forward_z), low(inverse_z), low(forward_x), low(inverse_x)


def gelu_parts(x):
    k = math.sqrt(2.0 / math.pi)
    sq = x * x
    t = jnp.tanh(k * x * (1.0 + 0.044715 * sq))
    half = 0.5 * (1.0 + t)
    slope = half + 0.5 * x * (1.0 - t * t) * (k * (1.0 + 3 * 0.044715 * sq))
    return x * half, slope


def dot(a, b, dims=((1,), (0,))):
    return lax.dot_general(a, b, (dims, ((), ())), preferred_element_type=F32)


NT = ((1,), (1,))
TN = ((0,), (0,))


def slabs_of(src, table, x, y0):
    low_lane = lax.broadcasted_iota(jnp.int32, (KZ, LANES), 1) < LANES // 2
    pieces = []
    for b in range(GROUP // 2):
        even = src[y0 + 2 * b, x].astype(F32)
        odd = src[y0 + 2 * b + 1, x].astype(F32)
        real = jnp.where(low_lane, even, pltpu.roll(odd, LANES // 2, 1))
        imag = jnp.where(low_lane, pltpu.roll(even, LANES // 2, 1), odd)
        pieces.append(jnp.concatenate([real, imag], 0))
    return dot(jnp.concatenate(pieces, 1).astype(BF16), table[...], TN)


def loop(low, high, step):
    if high - low <= 4:
        for i in range(low, high):
            step(i)
    else:
        lax.fori_loop(low, high, lambda i, c: (step(i), c)[1], 0)


def kernel(
    n, planes, rows, own, scale,
    field_hbm, cot_hbm, weight_hbm, tx_hbm, ti_hbm, w_in, w_out_t, fz, gz,
    out_field, out_spec, out_dw, out_coeffs,
    s1, r1, s4, r4, s5, r5, s8, r8,
    s2, r2, s3, r3, s6, r6, s7, r7,
    sw, rw, sg, rg,
    wfull, xs, ys, ds, act, slope, branch, dw,
    field, cot, weight, tx, ti,
    send_sem, recv_sem, load_sem,
):
    me = lax.axis_index("gx")
    loads = [
        pltpu.make_async_copy(src, dst, load_sem.at[i])
        for i, (src, dst) in enumerate((
            (field_hbm, field), (weight_hbm, weight), (tx_hbm, tx), (ti_hbm, ti), (cot_hbm, cot)))
    ]
    for load in loads:
        load.start()
    low_lane = lax.broadcasted_iota(jnp.int32, (KZ, LANES), 1) < LANES // 2
    chans = LANES // 2
    per_x = rows // GROUP
    groups = planes * per_x

    barrier = pltpu.get_barrier_semaphore()

    def greet(i, c):
        pl.semaphore_signal(barrier, inc=1, device_id={"gx": lax.rem(me + i, n)})
        return c

    lax.fori_loop(1, n, greet, 0)

    def send(phase, src, dst):
        def one(i, c):
            to = lax.rem(me + i, n)
            pltpu.make_async_remote_copy(
                src_ref=src(to), dst_ref=dst.at[me],
                send_sem=send_sem.at[phase], recv_sem=recv_sem.at[phase],
                device_id={"gx": to},
            ).start()
            return c

        lax.fori_loop(1, n, one, 0)

    def exchange(phase, src, dst):
        send(phase, lambda to: src.at[to], dst)
        dst[me] = src[me]

    def bulk(phase, dst):
        some = dst.at[pl.ds(0, n - 1)]
        return pltpu.make_async_remote_copy(
            src_ref=some, dst_ref=some,
            send_sem=send_sem.at[phase], recv_sem=recv_sem.at[phase],
            device_id={"gx": lax.rem(me + 1, n)},
        )

    def swap(v):
        return pltpu.roll(v, LANES // 2, 1)

    def rotated(v, first):
        lane = lax.broadcasted_iota(jnp.int32, v.shape, 1) < LANES // 2
        turned = swap(v)
        return jnp.where(lane, first * turned, -first * turned)

    def place(g):
        return g // per_x, lax.rem(g, per_x) * GROUP if not isinstance(g, int) else (g % per_x) * GROUP

    def z_forward(g, slabs, table, dst):
        res = dot(table[...], slabs, NT)
        x, y0 = place(g)
        for b in range(GROUP // 2):
            real = res[:KZ, b * LANES:(b + 1) * LANES]
            imag = res[KZ:, b * LANES:(b + 1) * LANES]
            dst[y0 + 2 * b, x] = jnp.where(low_lane, real, swap(imag)).astype(BF16)
            dst[y0 + 2 * b + 1, x] = jnp.where(low_lane, swap(real), imag).astype(BF16)

    def z_inverse(g, src, table):
        return slabs_of(src, table, *place(g))

    def x_forward(src, dst):
        data = src[...].reshape(n * planes * KZ, LANES)
        both = dot(tx[...], data)
        half = KX * KZ
        spec = both[:half] + rotated(both[half:], 1.0)
        for d in range(n):
            dst[d] = spec[d * own:(d + 1) * own].astype(dst.dtype)

    def x_inverse(src, dst):
        data = jnp.concatenate([src[d].astype(F32) for d in range(n)], 0).astype(BF16)
        both = dot(ti[...], data)
        half = n * planes * KZ
        res = both[:half] + rotated(both[half:], -1.0)
        dst[...] = res.astype(BF16).reshape(dst.shape)

    def spread(src, dst):
        for d in range(n):
            dst[d * own:(d + 1) * own, :] = src[d].astype(F32)

    def collect(src, dst):
        for d in range(n):
            dst[d] = src[d * own:(d + 1) * own, :].astype(dst.dtype)

    def to_lane(v):
        return jnp.concatenate([v[i * chans:(i + 1) * chans] for i in range(GROUP)], 1)

    def to_row(v):
        return jnp.concatenate([v[:, i * LANES:(i + 1) * LANES] for i in range(GROUP)], 0)

    def slab_rows(ref, g):
        return ref[pl.ds(g * GROUP, GROUP)].reshape(GROUP * chans, LANES)

    def network(g):
        u = to_lane(slab_rows(field, g))
        value, grad = gelu_parts(dot(w_in[...], u, TN))
        value = value.astype(BF16)
        act[g] = value
        slope[g] = grad.astype(BF16)
        branch[g] = to_row(dot(w_out_t[...], value))

    def network_part(i):
        loop(i * groups // 4, (i + 1) * groups // 4, network)

    loads[0].wait()
    loop(0, groups, lambda g: z_forward(g, slab_rows(field, g), fz, s1))
    pl.semaphore_wait(barrier, n - 1)
    exchange(0, s1, r1)
    loads[1].wait()
    for m in range(own):
        w = weight[m].astype(F32)
        wfull[m] = jnp.concatenate([w, rotated(w, -1.0)], 0).astype(BF16)
    network_part(0)
    for load in loads[2:]:
        load.wait()
    bulk(0, r1).wait_recv()
    x_forward(r1, s2)
    exchange(1, s2, r2)
    network_part(1)
    bulk(1, r2).wait_recv()
    spread(r2, xs)
    for m in range(own):
        at = pl.ds(m, n, stride=own)
        ys[at, :] = dot(xs[at, :].astype(BF16), wfull[m])
    collect(ys, s3)
    exchange(2, s3, r3)
    network_part(2)
    bulk(2, r3).wait_recv()
    x_inverse(r3, s4)
    exchange(3, s4, r4)
    network_part(3)
    bulk(3, r4).wait_recv()

    def point(g):
        pre = z_inverse(g, r4, gz) + branch[g]
        unused, grad = gelu_parts(pre)
        d_pre = (slab_rows(cot, g).astype(F32) * grad).astype(BF16)
        out_field[pl.ds(g * GROUP, GROUP)] = d_pre.reshape(GROUP, chans, LANES)
        z_forward(g, d_pre, gz, s5)

    loop(0, groups, point)
    exchange(4, s5, r5)
    dw[...] = jnp.zeros_like(dw)

    def network_back(g):
        d_pre = to_lane(slab_rows(out_field, g))
        d_act = (slope[g].astype(F32) * dot(w_out_t[...], d_pre, TN)).astype(BF16)
        du = to_row(dot(w_in[...], d_act))
        out_field[pl.ds(g * GROUP, GROUP)] = du.astype(BF16).reshape(GROUP, chans, LANES)
        u = to_lane(slab_rows(field, g))
        dw[:chans, :] += dot(u, d_act, NT)
        dw[chans:, :] += dot(d_pre, act[g], NT)

    loop(0, groups // 2, network_back)
    bulk(4, r5).wait_recv()
    x_forward(r5, s6)
    exchange(5, s6, r6)
    loop(groups // 2, groups, network_back)
    share = LANES // n
    for d in range(n):
        sw[d] = dw[d * share:(d + 1) * share, :]
    exchange(8, sw, rw)
    bulk(5, r6).wait_recv()
    spread(r6, ds)
    for m in range(own):
        at = pl.ds(m, n, stride=own)
        ys[at, :] = dot(ds[at, :].astype(BF16), wfull[m], NT)
    collect(ys, s7)
    exchange(6, s7, r7)
    for m in range(own):
        at = pl.ds(m, n, stride=own)
        full = dot(xs[at, :].astype(BF16), ds[at, :].astype(BF16), TN)
        out_spec[m] = full[:chans] + rotated(full[chans:], 1.0)
    bulk(8, rw).wait_recv()
    sg[0] = jnp.sum(rw[...], 0) * scale
    send(9, lambda to: sg.at[0], rg)
    rg[me] = sg[0]
    bulk(6, r7).wait_recv()
    x_inverse(r7, s8)
    exchange(7, s8, r8)
    bulk(9, rg).wait_recv()
    for d in range(n):
        out_dw[d * share:(d + 1) * share, :] = rg[d]
    bulk(7, r8).wait_recv()
    out_coeffs[...] = r8[...]
    for phase, dst in enumerate((r1, r2, r3, r4, r5, r6, r7, r8, rw, rg)):
        bulk(phase, dst).wait_send()


def finish_kernel(
    planes, rows, coeffs, network, spec, dw, fz, out_field, out_spec, out_win, out_wout_t
):
    chans = LANES // 2
    per_x = rows // GROUP
    out_spec[...] = spec[...]
    out_win[...] = dw[:chans, :]
    out_wout_t[...] = dw[chans:, :]

    def finish(g):
        x, y0 = g // per_x, (g % per_x if isinstance(g, int) else lax.rem(g, per_x)) * GROUP
        at = pl.ds(g * GROUP, GROUP)
        du = slabs_of(coeffs, fz, x, y0) + network[at].reshape(GROUP * chans, LANES).astype(F32)
        out_field[at] = du.astype(BF16).reshape(GROUP, chans, LANES)

    loop(0, planes * per_x, finish)


def body(in_field, cotangent, spec_weight, w_in, w_out):
    n = lax.axis_size("gx")
    planes, rows, chans, z_cells = in_field.shape
    own = spec_weight.shape[0]
    length_x = planes * n
    assert rows == n and z_cells == LANES and 2 * chans == LANES
    fz, gz, tx, ti = make_tables(length_x, z_cells)
    slabs = planes * rows
    groups = slabs // GROUP
    hidden = w_in.shape[1]
    wire = BF16 if own % 16 == 0 else F32
    big = pltpu.VMEM((n, planes, KZ, LANES), BF16)
    small = pltpu.VMEM((n, own, LANES), wire)
    share = LANES // n
    scratch = [big] * 8 + [small] * 8 + [
        pltpu.VMEM((n, share, LANES), F32),
        pltpu.VMEM((n, share, LANES), F32),
        pltpu.VMEM((1, share, LANES), F32),
        pltpu.VMEM((n, share, LANES), F32),
        pltpu.VMEM((own, LANES, LANES), BF16),
        pltpu.VMEM((n * own, LANES), F32),
        pltpu.VMEM((n * own, LANES), F32),
        pltpu.VMEM((n * own, LANES), F32),
        pltpu.VMEM((groups, hidden, GROUP * LANES), BF16),
        pltpu.VMEM((groups, hidden, GROUP * LANES), BF16),
        pltpu.VMEM((groups, GROUP * chans, LANES), F32),
        pltpu.VMEM((LANES, LANES), F32),
        pltpu.VMEM((slabs, chans, z_cells), BF16),
        pltpu.VMEM((slabs, chans, z_cells), BF16),
        pltpu.VMEM(spec_weight.shape, BF16),
        pltpu.VMEM(tx.shape, BF16),
        pltpu.VMEM(ti.shape, BF16),
        pltpu.SemaphoreType.DMA((PHASES,)),
        pltpu.SemaphoreType.DMA((PHASES,)),
        pltpu.SemaphoreType.DMA((5,)),
    ]
    scale = 1.0 / math.sqrt(length_x * rows * z_cells)
    vmem = pl.BlockSpec(memory_space=pltpu.VMEM)
    hbm = pl.BlockSpec(memory_space=pl.ANY)
    field_shape = jax.ShapeDtypeStruct((slabs, chans, z_cells), BF16)
    spec_shape = jax.ShapeDtypeStruct(spec_weight.shape, F32)
    fz, gz = jnp.asarray(fz), jnp.asarray(gz)
    network, spec, dw, coeffs = pl.pallas_call(
        functools.partial(kernel, n, planes, rows, own, scale),
        out_shape=(
            field_shape,
            spec_shape,
            jax.ShapeDtypeStruct((LANES, LANES), F32),
            jax.ShapeDtypeStruct((n, planes, KZ, LANES), BF16),
        ),
        in_specs=[hbm] * 5 + [vmem] * 4,
        out_specs=(vmem,) * 4,
        scratch_shapes=scratch,
        compiler_params=pltpu.CompilerParams(
            collective_id=0, has_side_effects=True, vmem_limit_bytes=60 * 1024 * 1024
        ),
    )(
        in_field.reshape(slabs, chans, z_cells),
        cotangent.reshape(slabs, chans, z_cells),
        spec_weight, jnp.asarray(tx), jnp.asarray(ti), w_in, w_out.T, fz, gz,
    )
    grad_field, grad_spec, grad_w_in, grad_w_out_t = pl.pallas_call(
        functools.partial(finish_kernel, planes, rows),
        out_shape=(
            field_shape,
            spec_shape,
            jax.ShapeDtypeStruct(w_in.shape, F32),
            jax.ShapeDtypeStruct(w_out.shape[::-1], F32),
        ),
        in_specs=[vmem] * 5,
        out_specs=(vmem,) * 4,
        compiler_params=pltpu.CompilerParams(vmem_limit_bytes=63 * 1024 * 1024),
    )(coeffs, network, spec, dw, fz)
    return grad_field.reshape(in_field.shape), grad_spec, grad_w_in, grad_w_out_t.T


def solution(mesh):
    placed = (
        P(("rep", "gx"), None, None, None),
        P(("rep", "gx"), None, None, None),
        P("gx", None, None),
        P(),
        P(),
    )
    return jax.shard_map(
        body,
        mesh=mesh,
        in_specs=placed,
        out_specs=(
            P(("rep", "gx"), None, None, None),
            P(("rep", "gx"), None, None),
            P("rep", None),
            P("rep", None),
        ),
        check_vma=False,
    )
```
